256 devices in a mesh: dp: 16 (over x, z_lo, core), row: 4 (over y), col: 4 (over z_hi).
Axes of the slice: x: 4, y: 4, z: 8 (z_hi: 4, z_lo: 2; z = z_hi * 2 + z_lo), core: 2. Of those that a mesh axis runs over, the one named last changes fastest.
Arguments:
- tokens: bfloat16 [256, 12288], P(('dp', 'col'), 'row'), may hold values from -6 to 6
- cotangent: bfloat16 [256, 12288], P(('dp', 'col'), 'row'), may hold values from -1.796875 to 1.796875
- w_in: bfloat16 [12288, 24576], P('row', ('dp', 'col')), may hold values from -0.0546875 to 0.0546875
- w_out: bfloat16 [24576, 12288], P(('dp', 'col'), 'row'), may hold values from -0.0390625 to 0.0390625
Outputs:
- layer_output: bfloat16 [256, 12288], P(('dp', 'col'), 'row')
- input_grad: bfloat16 [256, 12288], P(('dp', 'col'), 'row')
- w_in_grad: bfloat16 [12288, 24576], P('row', ('dp', 'col'))
- w_out_grad: bfloat16 [24576, 12288], P(('dp', 'col'), 'row')
The draws below stay inside these ranges and needn't reach their ends.
All inputs are finite; a program needn't handle non-finite values.
Results may differ from the reference program's by a relative error of at most 0.017.
Values may be sent and summed in bfloat16 or wider, within the bound.
No kernel may reach another device: no remote copies, remote signals or barrier semaphores. Data moves between devices by JAX's collectives and lax.ppermute only.
A program may use at most 64 MiB of HBM per device.

```python
import jax
import jax.numpy as jnp

D = 12288
FFW = 24576
TOKENS = 256


def block_levels(key, dims, split, low, top_value):
    def one(dim, blocks):
        heights = jax.random.uniform(jax.random.fold_in(jax.random.fold_in(key, 6), dim), (blocks,), jnp.float32, low / len(split), top_value / len(split))
        return jnp.repeat(jnp.exp(heights), dims[dim] // blocks).reshape((-1,) + (1,) * (len(dims) - dim - 1))

    loudness = one(*split[0])
    for cut in split[1:]:
        loudness = loudness * one(*cut)
    return loudness


def centred(rng, dims, width, bound, split=(), dtype=jnp.bfloat16):
    entries = jax.random.normal(rng, dims, jnp.float32) * width
    if len(split) > 0:
        entries = block_levels(rng, dims, split, -0.22, 0.18) * entries
    return jnp.clip(entries, min=-bound, max=bound).astype(dtype)


def setup_inputs(seed: int = 0) -> dict:
    keys = jax.random.split(jax.random.key(seed), 5)
    return {
        "tokens": centred(keys[0], (TOKENS, D), 1.0, 6.0, ((0, 64), (1, 4))),
        "cotangent": centred(keys[1], (TOKENS, D), 0.3, 1.796875, ((0, 64), (1, 4))),
        "w_in": centred(keys[2], (D, FFW), D ** -0.5, 0.0546875, ((0, 4), (1, 64))),
        "w_out": centred(keys[3], (FFW, D), FFW ** -0.5, 0.0390625, ((0, 64), (1, 4))),
    }


SQRT_TWO_PI = 0.7978845608028654
CUBIC = 0.044715


def gelu_value(preact):
    inner = SQRT_TWO_PI * (preact + CUBIC * preact * preact * preact)
    return 0.5 * preact * (1.0 + jnp.tanh(inner))


def gelu_slope(preact):
    tangent = jnp.tanh(SQRT_TWO_PI * (preact + CUBIC * preact * preact * preact))
    return 0.5 * (1.0 + tangent) + 0.5 * preact * (1.0 - tangent * tangent) * SQRT_TWO_PI * (1.0 + 3.0 * CUBIC * preact * preact)


def reference(tokens, cotangent, w_in, w_out):
    preact = jnp.dot(tokens, w_in, preferred_element_type=jnp.float32)
    activated = gelu_value(preact).astype(jnp.bfloat16)
    layer_output = jnp.dot(activated, w_out, preferred_element_type=jnp.float32).astype(jnp.bfloat16)
    grad_act = jnp.dot(cotangent, w_out.T, preferred_element_type=jnp.float32)
    grad_pre = (grad_act * gelu_slope(preact)).astype(jnp.bfloat16)
    input_grad = jnp.dot(grad_pre, w_in.T, preferred_element_type=jnp.float32).astype(jnp.bfloat16)
    w_in_grad = jnp.dot(tokens.T, grad_pre, preferred_element_type=jnp.float32).astype(jnp.bfloat16)
    w_out_grad = jnp.dot(activated.T, cotangent, preferred_element_type=jnp.float32).astype(jnp.bfloat16)
    return (layer_output, input_grad, w_in_grad, w_out_grad)
```

```python
import jax
import jax.numpy as jnp
from jax import lax
from jax.sharding import PartitionSpec as P

SQRT_TWO_PI = 0.7978845608028654
CUBIC = 0.044715
PLANE = ("dp", "col")
NX, NZ, NC = 4, 8, 2
BF16, F32 = jnp.bfloat16, jnp.float32


def place(flat):
    dp, z_hi = divmod(flat, 4)
    return dp // 4, z_hi * 2 + (dp // 2) % 2, dp % 2


def index(x, z, core):
    x, z, core = x % NX, z % NZ, core % NC
    return ((x * 2 + z % 2) * 2 + core) * 4 + z // 2


def pairs(source_of):
    return [(index(*source_of(*place(f))), f) for f in range(NX * NZ * NC)]


def inverse(perm):
    return [(b, a) for a, b in perm]


OTHER_CORE = pairs(lambda x, z, c: (x, z, c + 1))
Z_SLOTS = [pairs(lambda x, z, c: (x, z + 4 * c, c))] + [
    pairs(lambda x, z, c, d=d: (x, z + (d if c == 0 else -d), c)) for d in (1, 2, 3)
]
X_SLOTS = [pairs(lambda x, z, c, d=d: (x + d, z, c)) for d in (1, 2, 3)]
ROW_SHIFTS = [[(i, (i + d) % 4) for i in range(4)] for d in (1, 2, 3)]


def send(value, perm):
    return lax.ppermute(value, PLANE, perm)


def gelu_both(preact):
    tangent = jnp.tanh(SQRT_TWO_PI * (preact + CUBIC * preact * preact * preact))
    value = 0.5 * preact * (1.0 + tangent)
    slope = 0.5 * (1.0 + tangent) + 0.5 * preact * (1.0 - tangent * tangent) * SQRT_TWO_PI * (
        1.0 + 3.0 * CUBIC * preact * preact
    )
    return value, slope


def collect_x(share):
    own = jnp.concatenate([share] + [send(share, p) for p in X_SLOTS], axis=0)
    return own, send(own, OTHER_CORE)


def sum_rows(part):
    rounded = part.astype(BF16)
    for shift in ROW_SHIFTS:
        part = part + lax.ppermute(rounded, "row", shift).astype(F32)
    return part


def reduce_x(part):
    half = part.shape[0] // 2
    total = part[:half] + send(part[half:].astype(BF16), OTHER_CORE).astype(F32)
    rows = half // NX
    rounded = total[rows:].astype(BF16)
    total = total[:rows]
    for i, perm in enumerate(X_SLOTS):
        total = total + send(rounded[i * rows : (i + 1) * rows], inverse(perm)).astype(F32)
    return total


def on_device(tokens, cotangent, w_in, w_out):
    width = tokens.shape[1]
    mine = jnp.stack([tokens, cotangent])
    block = jnp.concatenate([mine, send(mine, OTHER_CORE)], axis=1)
    share = jnp.concatenate([send(block, p) for p in Z_SLOTS], axis=1)

    x_own, x_other = collect_x(share[0])
    g_own, g_other = collect_x(share[1])
    x_whole = jnp.concatenate([x_own, x_other], axis=0)
    g_whole = jnp.concatenate([g_own, g_other], axis=0)

    preact = sum_rows(jnp.dot(x_whole, w_in, preferred_element_type=F32))
    value, slope = gelu_both(preact)
    activated = value.astype(BF16)
    forward = reduce_x(jnp.dot(activated, w_out, preferred_element_type=F32))

    grad_act = sum_rows(
        lax.dot_general(g_whole, w_out, (((1,), (1,)), ((), ())), preferred_element_type=F32)
    )
    grad_pre = (grad_act * slope).astype(BF16)
    backward = reduce_x(
        lax.dot_general(grad_pre, w_in, (((1,), (1,)), ((), ())), preferred_element_type=F32)
    )

    w_in_grad = lax.dot_general(
        x_whole, grad_pre, (((0,), (0,)), ((), ())), preferred_element_type=F32
    ).astype(BF16)
    w_out_grad = lax.dot_general(
        activated, g_whole, (((0,), (0,)), ((), ())), preferred_element_type=F32
    ).astype(BF16)

    both = jnp.stack([forward, backward]).astype(BF16)
    summed = jnp.zeros((2, 8, width), F32)
    for i, perm in enumerate(Z_SLOTS):
        summed = summed + send(both[:, 8 * i : 8 * i + 8], inverse(perm)).astype(F32)
    summed = summed[:, :4] + send(summed[:, 4:], OTHER_CORE)
    layer_output, input_grad = summed[0].astype(BF16), summed[1].astype(BF16)
    return (layer_output, input_grad, w_in_grad, w_out_grad)


def solution(mesh):
    in_specs = (
        P(PLANE, "row"),
        P(PLANE, "row"),
        P("row", PLANE),
        P(PLANE, "row"),
    )
    out_specs = (
        P(PLANE, "row"),
        P(PLANE, "row"),
        P("row", PLANE),
        P(PLANE, "row"),
    )
    return jax.shard_map(
        on_device, mesh=mesh, in_specs=in_specs, out_specs=out_specs, check_vma=False
    )
```

```python
import functools

import jax
import jax.numpy as jnp
from jax import lax
from jax.experimental import pallas as pl
from jax.experimental.pallas import tpu as pltpu
from jax.sharding import PartitionSpec as P

SQRT_TWO_PI = 0.7978845608028654
CUBIC = 0.044715
PLANE = ("dp", "col")
NX, NZ, NC = 4, 8, 2
BF16, F32 = jnp.bfloat16, jnp.float32
FLOPS = 4 * 10**9


def place(flat):
    dp, z_hi = divmod(flat, 4)
    return dp // 4, z_hi * 2 + (dp // 2) % 2, dp % 2


def index(x, z, core):
    x, z, core = x % NX, z % NZ, core % NC
    return ((x * 2 + z % 2) * 2 + core) * 4 + z // 2


def pairs(source_of):
    return [(index(*source_of(*place(f))), f) for f in range(NX * NZ * NC)]


def inverse(perm):
    return [(b, a) for a, b in perm]


OTHER_CORE = pairs(lambda x, z, c: (x, z, c + 1))
Z_SLOTS = [pairs(lambda x, z, c: (x, z + 4 * c, c))] + [
    pairs(lambda x, z, c, d=d: (x, z + (d if c == 0 else -d), c)) for d in (1, 2, 3)
]
X_NEXT = pairs(lambda x, z, c: (x + 1 - 2 * c, z, c))
X_FAR = pairs(lambda x, z, c: (x + 2, z, c))
ROW_SHIFTS = [[(i, (i + d) % 4) for i in range(4)] for d in (1, 2, 3)]


def send(value, perm):
    return lax.ppermute(value, PLANE, perm)


def gelu_both(preact):
    tangent = jnp.tanh(SQRT_TWO_PI * (preact + CUBIC * preact * preact * preact))
    value = 0.5 * preact * (1.0 + tangent)
    slope = 0.5 * (1.0 + tangent) + 0.5 * preact * (1.0 - tangent * tangent) * SQRT_TWO_PI * (
        1.0 + 3.0 * CUBIC * preact * preact
    )
    return value, slope


def after(value, *others):
    return lax.optimization_barrier((value,) + others)[0]


def exchange_rows(rounded):
    return [lax.ppermute(rounded, "row", shift) for shift in ROW_SHIFTS]


def total(part, received):
    for piece in received:
        part = part + piece.astype(F32)
    return part


def gather_x(share, both):
    return [share, send(both, X_NEXT), send(share, X_FAR)]


def finish_x(own, back):
    near, far = back
    rows = own.shape[0]
    across = send(near[rows:], OTHER_CORE)
    return total(own, [near[:rows], far, across]).astype(BF16)


def dot(a, b):
    return jnp.dot(a, b, preferred_element_type=F32)


def dot_t(a, b):
    return lax.dot_general(a, b, (((1,), (1,)), ((), ())), preferred_element_type=F32)


def t_dot(a, b):
    return lax.dot_general(a, b, (((0,), (0,)), ((), ())), preferred_element_type=F32)


def rows_of(pieces):
    return jnp.concatenate(pieces, axis=0)


CHUNK = 768


def cuts(size):
    return [slice(k, k + CHUNK) for k in range(0, size, CHUNK)]


def inward(transposed, own, near, far, w_a, w_b, part, rounded):
    units = part.shape[1] // 2
    for i, w in enumerate((w_a, w_b)):
        total = 0.0
        for cut in cuts(own.shape[1]):
            rows = rows_of([own[:, cut], near[:, cut], far[:, cut]])
            total = total + (dot_t(rows, w[:, cut]) if transposed else dot(rows, w[cut, :]))
        columns = slice(i * units, (i + 1) * units)
        part[:, columns] = total
        rounded[:, columns] = total.astype(BF16)


def outward(transposed, hidden, w_a, w_b, own, near, far):
    units = hidden.shape[1] // 2
    a, b = hidden[:, :units], hidden[:, units:]
    n_own, n_near = own.shape[0], near.shape[0]
    for cut in cuts(own.shape[1]):
        if transposed:
            out = dot_t(a, w_a[cut, :]) + dot_t(b, w_b[cut, :])
        else:
            out = dot(a, w_a[:, cut]) + dot(b, w_b[:, cut])
        own[:, cut] = out[:n_own]
        near[:, cut] = out[n_own : n_own + n_near].astype(BF16)
        far[:, cut] = out[n_own + n_near :].astype(BF16)


def forward_body(part, r0, r1, r2, w_a, w_b, activated, slope, own, near, far):
    preact = part[...]
    for r in (r0, r1, r2):
        preact = preact + r[...].astype(F32)
    value, slope[...] = gelu_both(preact)
    hidden = value.astype(BF16)
    activated[...] = hidden
    outward(False, hidden, w_a, w_b, own, near, far)


def backward_body(part, r0, r1, r2, slope, w_a, w_b, grad_pre, own, near, far):
    grad = part[...]
    for r in (r0, r1, r2):
        grad = grad + r[...].astype(F32)
    hidden = (grad * slope[...]).astype(BF16)
    grad_pre[...] = hidden
    outward(True, hidden, w_a, w_b, own, near, far)


def call(body, values, outs, flops=0):
    vmem = pl.BlockSpec(memory_space=pltpu.VMEM)
    return pl.pallas_call(
        body,
        out_shape=[jax.ShapeDtypeStruct(shape, dtype) for shape, dtype in outs],
        in_specs=[vmem] * len(values),
        out_specs=[vmem] * len(outs),
        compiler_params=pltpu.CompilerParams(vmem_limit_bytes=32 * 2**20),
        cost_estimate=pl.CostEstimate(flops=flops, bytes_accessed=0, transcendentals=0),
    )(*values)


def on_device(tokens, cotangent, w_in, w_out):
    width, units = w_in.shape
    mine = jnp.stack([tokens, cotangent])
    block = jnp.concatenate([mine, send(mine, OTHER_CORE)], axis=1)
    share = jnp.concatenate([send(block, p) for p in Z_SLOTS], axis=1)
    across = send(share, OTHER_CORE)
    both = jnp.concatenate([share, across], axis=1)

    x_pieces = gather_x(share[0], both[0])
    w_in_other = send(after(w_in, across), OTHER_CORE)
    w_out_other = send(after(w_out, across), OTHER_CORE)
    rows, hidden_shape = 4 * share.shape[1], (4 * share.shape[1], 2 * units)
    outgoing = [((rows // 4, width), F32), ((rows // 2, width), BF16), ((rows // 4, width), BF16)]
    g_pieces = gather_x(share[1], both[1])
    hidden_out = [(hidden_shape, F32), (hidden_shape, BF16)]

    inner_part, rounded = call(
        functools.partial(inward, False), x_pieces + [w_in, w_in_other], hidden_out, FLOPS
    )
    inner_rest = exchange_rows(rounded)
    g_pieces = [after(piece, inner_part) for piece in g_pieces]
    back_part, rounded = call(
        functools.partial(inward, True), g_pieces + [w_out, w_out_other], hidden_out
    )
    back_rest = exchange_rows(rounded)

    inner_rest = [after(piece, back_part) for piece in inner_rest]
    activated, slope, forward, near, far = call(
        forward_body, [inner_part] + inner_rest + [w_out, w_out_other],
        [(hidden_shape, BF16), (hidden_shape, F32)] + outgoing,
    )
    forward_rest = send(near, inverse(X_NEXT)), send(far, inverse(X_FAR))
    grad_pre, backward, near, far = call(
        backward_body, [back_part] + back_rest + [slope, w_in, w_in_other],
        [(hidden_shape, BF16)] + outgoing,
    )
    backward_rest = send(near, inverse(X_NEXT)), send(far, inverse(X_FAR))
    forward = finish_x(forward, [after(piece, backward) for piece in forward_rest])

    x_own, g_own = rows_of(x_pieces), rows_of(g_pieces)
    rest = after(jnp.stack([x_own[32:], g_own[32:]]), backward)
    rest = send(rest, OTHER_CORE)
    hidden = jnp.stack([activated[:, :units], grad_pre[:, :units]])
    hidden_rest = send(jnp.stack([activated[:, units:], grad_pre[:, units:]]), OTHER_CORE)
    x_whole = rows_of([x_own, across[0], rest[0]])
    g_whole = rows_of([g_own, across[1], rest[1]])
    w_out_grad = t_dot(rows_of([hidden[0], hidden_rest[0]]), g_whole).astype(BF16)
    w_in_grad = t_dot(x_whole, rows_of([hidden[1], hidden_rest[1]])).astype(BF16)

    backward_rest = [after(piece, w_in_grad, w_out_grad, forward) for piece in backward_rest]
    backward = finish_x(backward, backward_rest)
    result = jnp.stack([forward, backward])
    summed = jnp.zeros((2, 8, width), F32)
    for i, perm in enumerate(Z_SLOTS):
        summed = summed + send(result[:, 8 * i : 8 * i + 8], inverse(perm)).astype(F32)
    summed = summed[:, :4] + send(summed[:, 4:].astype(BF16), OTHER_CORE).astype(F32)
    layer_output, input_grad = summed[0].astype(BF16), summed[1].astype(BF16)
    return (layer_output, input_grad, w_in_grad, w_out_grad)


def solution(mesh):
    in_specs = (
        P(PLANE, "row"),
        P(PLANE, "row"),
        P("row", PLANE),
        P(PLANE, "row"),
    )
    out_specs = (
        P(PLANE, "row"),
        P(PLANE, "row"),
        P("row", PLANE),
        P(PLANE, "row"),
    )
    return jax.shard_map(
        on_device, mesh=mesh, in_specs=in_specs, out_specs=out_specs, check_vma=False
    )
```

```python
import functools

import jax
import jax.numpy as jnp
from jax import lax
from jax.experimental import pallas as pl
from jax.experimental.pallas import tpu as pltpu
from jax.sharding import PartitionSpec as P

SQRT_TWO_PI = 0.7978845608028654
CUBIC = 0.044715
PLANE = ("dp", "col")
NX, NZ, NC = 4, 8, 2
BF16, F32 = jnp.bfloat16, jnp.float32
FLOPS = 4 * 10**9


def place(flat):
    dp, z_hi = divmod(flat, 4)
    return dp // 4, z_hi * 2 + (dp // 2) % 2, dp % 2


def index(x, z, core):
    x, z, core = x % NX, z % NZ, core % NC
    return ((x * 2 + z % 2) * 2 + core) * 4 + z // 2


def pairs(source_of):
    return [(index(*source_of(*place(f))), f) for f in range(NX * NZ * NC)]


def inverse(perm):
    return [(b, a) for a, b in perm]


OTHER_CORE = pairs(lambda x, z, c: (x, z, c + 1))
Z_SLOTS = [pairs(lambda x, z, c: (x, z + 4 * c, c))] + [
    pairs(lambda x, z, c, d=d: (x, z + (d if c == 0 else -d), c)) for d in (1, 2, 3)
]
X_NEXT = pairs(lambda x, z, c: (x + 1 - 2 * c, z, c))
X_FAR = pairs(lambda x, z, c: (x + 2, z, c))
ROW_SHIFTS = [[(i, (i + d) % 4) for i in range(4)] for d in (1, 2, 3)]


def send(value, perm):
    return lax.ppermute(value, PLANE, perm)


def gelu_both(preact):
    tangent = jnp.tanh(SQRT_TWO_PI * (preact + CUBIC * preact * preact * preact))
    value = 0.5 * preact * (1.0 + tangent)
    slope = 0.5 * (1.0 + tangent) + 0.5 * preact * (1.0 - tangent * tangent) * SQRT_TWO_PI * (
        1.0 + 3.0 * CUBIC * preact * preact
    )
    return value, slope


def after(value, *others):
    return lax.optimization_barrier((value,) + others)[0]


def exchange_rows(rounded):
    return [lax.ppermute(rounded, "row", shift) for shift in ROW_SHIFTS]


def total(part, received):
    for piece in received:
        part = part + piece.astype(F32)
    return part


def gather_x(share, both):
    return [share, send(both, X_NEXT), send(share, X_FAR)]


def finish_x(own, back):
    near, far = back
    rows = own.shape[0]
    across = send(near[rows:], OTHER_CORE)
    return total(own, [near[:rows], far, across]).astype(BF16)


def dot(a, b):
    return jnp.dot(a, b, preferred_element_type=F32)


def dot_t(a, b):
    return lax.dot_general(a, b, (((1,), (1,)), ((), ())), preferred_element_type=F32)


def t_dot(a, b):
    return lax.dot_general(a, b, (((0,), (0,)), ((), ())), preferred_element_type=F32)


def columns_of(pieces):
    return jnp.concatenate(pieces, axis=1)


def split_rows(value, count):
    rows = value.shape[0] // count
    return [value[i * rows : (i + 1) * rows] for i in range(count)]


def rows_of(pieces):
    return jnp.concatenate(pieces, axis=0)


CHUNK = 768


def cuts(size):
    return [slice(k, k + CHUNK) for k in range(0, size, CHUNK)]


def inward(transposed, own, near, far, w_a, w_b, part, rounded):
    units = part.shape[1] // 2
    for i, w in enumerate((w_a, w_b)):
        total = 0.0
        for cut in cuts(own.shape[1]):
            rows = rows_of([own[:, cut], near[:, cut], far[:, cut]])
            total = total + (dot_t(rows, w[:, cut]) if transposed else dot(rows, w[cut, :]))
        columns = slice(i * units, (i + 1) * units)
        part[:, columns] = total
        rounded[:, columns] = total.astype(BF16)


def outward(transposed, hidden, w_a, w_b, own, near, far):
    units = hidden.shape[1] // 2
    a, b = hidden[:, :units], hidden[:, units:]
    n_own, n_near = own.shape[0], near.shape[0]
    for cut in cuts(own.shape[1]):
        if transposed:
            out = dot_t(a, w_a[cut, :]) + dot_t(b, w_b[cut, :])
        else:
            out = dot(a, w_a[:, cut]) + dot(b, w_b[:, cut])
        own[:, cut] = out[:n_own]
        near[:, cut] = out[n_own : n_own + n_near].astype(BF16)
        far[:, cut] = out[n_own + n_near :].astype(BF16)


def forward_body(part, r0, r1, r2, w_a, w_b, activated, slope, own, near, far):
    preact = part[...]
    for r in (r0, r1, r2):
        preact = preact + r[...].astype(F32)
    value, slope[...] = gelu_both(preact)
    hidden = value.astype(BF16)
    activated[...] = hidden
    outward(False, hidden, w_a, w_b, own, near, far)


def backward_body(part, r0, r1, r2, slope, w_a, w_b, grad_pre, own, near, far):
    grad = part[...]
    for r in (r0, r1, r2):
        grad = grad + r[...].astype(F32)
    hidden = (grad * slope[...]).astype(BF16)
    grad_pre[...] = hidden
    outward(True, hidden, w_a, w_b, own, near, far)


def call(body, values, outs, flops=0):
    vmem = pl.BlockSpec(memory_space=pltpu.VMEM)
    return pl.pallas_call(
        body,
        out_shape=[jax.ShapeDtypeStruct(shape, dtype) for shape, dtype in outs],
        in_specs=[vmem] * len(values),
        out_specs=[vmem] * len(outs),
        compiler_params=pltpu.CompilerParams(vmem_limit_bytes=32 * 2**20),
        cost_estimate=pl.CostEstimate(flops=flops, bytes_accessed=0, transcendentals=0),
    )(*values)


def on_device(tokens, cotangent, w_in, w_out):
    width, units = w_in.shape
    mine = jnp.stack([tokens, cotangent])
    block = jnp.concatenate([mine, send(mine, OTHER_CORE)], axis=1)
    slots = [send(block, p) for p in Z_SLOTS]
    w_in_other = send(after(w_in, slots[1]), OTHER_CORE)
    w_out_other = send(after(w_out, slots[2]), OTHER_CORE)
    share = jnp.concatenate(slots, axis=1)
    across = send(share, OTHER_CORE)
    both = jnp.concatenate([share, across], axis=1)

    x_pieces = gather_x(share[0], both[0])
    rows, hidden_shape = 4 * share.shape[1], (4 * share.shape[1], 2 * units)
    outgoing = [((rows // 4, width), F32), ((rows // 2, width), BF16), ((rows // 4, width), BF16)]
    g_near = send(both[1], X_NEXT)
    hidden_out = [(hidden_shape, F32), (hidden_shape, BF16)]

    inner_part, rounded = call(
        functools.partial(inward, False), x_pieces + [w_in, w_in_other], hidden_out, FLOPS
    )
    inner_rest = exchange_rows(rounded)
    g_near = after(g_near, inner_part)
    g_pieces = [share[1], g_near, send(g_near[: share.shape[1]], X_NEXT)]
    back_part, rounded = call(
        functools.partial(inward, True), g_pieces + [w_out, w_out_other], hidden_out
    )
    back_rest = exchange_rows(rounded)

    inner_rest = [after(piece, back_part) for piece in inner_rest]
    activated, slope, forward, near, far = call(
        forward_body, [inner_part] + inner_rest + [w_out, w_out_other],
        [(hidden_shape, BF16), (hidden_shape, F32)] + outgoing,
    )
    forward_rest = send(near, inverse(X_NEXT)), send(far, inverse(X_FAR))
    grad_pre, backward, near, far = call(
        backward_body, [back_part] + back_rest + [slope, w_in, w_in_other],
        [(hidden_shape, BF16)] + outgoing,
    )
    backward_rest = send(near, inverse(X_NEXT)), send(far, inverse(X_FAR))
    forward = finish_x(forward, [after(piece, backward) for piece in forward_rest])

    x_rest, g_rest = (rows_of(pieces[1:]) for pieces in (x_pieces, g_pieces))
    rest = [
        rows_of([kept, columns_of(split_rows(hidden[:, units:], 8))])
        for kept, hidden in ((x_rest, grad_pre), (g_rest, activated))
    ]
    rest = send(jnp.stack(rest), OTHER_CORE)
    kept = x_rest.shape[0]

    def with_other(share, mine, across, hidden, other):
        hidden_other = rows_of([other[kept:, i * units : (i + 1) * units] for i in range(8)])
        return rows_of([share, mine, across, other[:kept]]), rows_of([hidden[:, :units], hidden_other])

    x_whole, pre_whole = with_other(share[0], x_rest, across[0], grad_pre, rest[0])
    g_whole, act_whole = with_other(share[1], g_rest, across[1], activated, rest[1])
    w_out_grad = t_dot(act_whole, g_whole).astype(BF16)
    w_in_grad = t_dot(x_whole, pre_whole).astype(BF16)

    backward_rest = [after(piece, w_in_grad, w_out_grad, forward) for piece in backward_rest]
    backward = finish_x(backward, backward_rest)
    result = jnp.stack([forward, backward])
    summed = jnp.zeros((2, 8, width), F32)
    for i in (1, 2, 3, 0):
        piece = send(result[:, 8 * i : 8 * i + 8], inverse(Z_SLOTS[i]))
        summed = summed + piece.astype(F32)
    summed = summed[:, :4] + send(summed[:, 4:].astype(BF16), OTHER_CORE).astype(F32)
    layer_output, input_grad = summed[0].astype(BF16), summed[1].astype(BF16)
    return (layer_output, input_grad, w_in_grad, w_out_grad)


def solution(mesh):
    in_specs = (
        P(PLANE, "row"),
        P(PLANE, "row"),
        P("row", PLANE),
        P(PLANE, "row"),
    )
    out_specs = (
        P(PLANE, "row"),
        P(PLANE, "row"),
        P("row", PLANE),
        P(PLANE, "row"),
    )
    return jax.shard_map(
        on_device, mesh=mesh, in_specs=in_specs, out_specs=out_specs, check_vma=False
    )
```

```python
import functools

import jax
import jax.numpy as jnp
from jax import lax
from jax.experimental import pallas as pl
from jax.experimental.pallas import tpu as pltpu
from jax.sharding import PartitionSpec as P

SQRT_TWO_PI = 0.7978845608028654
CUBIC = 0.044715
PLANE = ("dp", "col")
NX, NZ, NC = 4, 8, 2
BF16, F32 = jnp.bfloat16, jnp.float32
FLOPS = 4 * 10**9


def place(flat):
    dp, z_hi = divmod(flat, 4)
    return dp // 4, z_hi * 2 + (dp // 2) % 2, dp % 2


def index(x, z, core):
    x, z, core = x % NX, z % NZ, core % NC
    return ((x * 2 + z % 2) * 2 + core) * 4 + z // 2


def pairs(source_of):
    return [(index(*source_of(*place(f))), f) for f in range(NX * NZ * NC)]


def inverse(perm):
    return [(b, a) for a, b in perm]


OTHER_CORE = pairs(lambda x, z, c: (x, z, c + 1))
Z_SLOTS = [pairs(lambda x, z, c: (x, z + 4 * c, c))] + [
    pairs(lambda x, z, c, d=d: (x, z + (d if c == 0 else -d), c)) for d in (1, 2, 3)
]
X_NEXT = pairs(lambda x, z, c: (x + 1 - 2 * c, z, c))
X_FAR = pairs(lambda x, z, c: (x + 2, z, c))
ROW_SHIFTS = [[(i, (i + d) % 4) for i in range(4)] for d in (2, 3, 1)]


def send(value, perm):
    return lax.ppermute(value, PLANE, perm)


def gelu_both(preact):
    tangent = jnp.tanh(SQRT_TWO_PI * (preact + CUBIC * preact * preact * preact))
    value = 0.5 * preact * (1.0 + tangent)
    slope = 0.5 * (1.0 + tangent) + 0.5 * preact * (1.0 - tangent * tangent) * SQRT_TWO_PI * (
        1.0 + 3.0 * CUBIC * preact * preact
    )
    return value, slope


def after(value, *others):
    return lax.optimization_barrier((value,) + others)[0]


def exchange_rows(rounded):
    return [lax.ppermute(rounded, "row", shift) for shift in ROW_SHIFTS]


def total(part, received):
    for piece in received:
        part = part + piece.astype(F32)
    return part


def gather_x(share, both):
    return [share, send(both, X_NEXT), send(share, X_FAR)]


def finish_x(own, back):
    near, far = back
    rows = own.shape[0]
    across = send(near[rows:], OTHER_CORE)
    return total(own, [near[:rows], far, across]).astype(BF16)


def dot(a, b):
    return jnp.dot(a, b, preferred_element_type=F32)


def dot_t(a, b):
    return lax.dot_general(a, b, (((1,), (1,)), ((), ())), preferred_element_type=F32)


def t_dot(a, b):
    return lax.dot_general(a, b, (((0,), (0,)), ((), ())), preferred_element_type=F32)


def columns_of(pieces):
    return jnp.concatenate(pieces, axis=1)


def split_rows(value, count):
    rows = value.shape[0] // count
    return [value[i * rows : (i + 1) * rows] for i in range(count)]


def rows_of(pieces):
    return jnp.concatenate(pieces, axis=0)


CHUNK = 768


def cuts(size):
    return [slice(k, k + CHUNK) for k in range(0, size, CHUNK)]


def inward(transposed, own, near, far, w_a, w_b, part, rounded):
    units = part.shape[1] // 2
    for i, w in enumerate((w_a, w_b)):
        total = 0.0
        for cut in cuts(own.shape[1]):
            rows = rows_of([own[:, cut], near[:, cut], far[:, cut]])
            total = total + (dot_t(rows, w[:, cut]) if transposed else dot(rows, w[cut, :]))
        columns = slice(i * units, (i + 1) * units)
        part[:, columns] = total
        rounded[:, columns] = total.astype(BF16)


def outward(transposed, hidden, w_a, w_b, own, near, far):
    units = hidden.shape[1] // 2
    a, b = hidden[:, :units], hidden[:, units:]
    n_own, n_near = own.shape[0], near.shape[0]
    for cut in cuts(own.shape[1]):
        if transposed:
            out = dot_t(a, w_a[cut, :]) + dot_t(b, w_b[cut, :])
        else:
            out = dot(a, w_a[:, cut]) + dot(b, w_b[:, cut])
        own[:, cut] = out[:n_own]
        near[:, cut] = out[n_own : n_own + n_near].astype(BF16)
        far[:, cut] = out[n_own + n_near :].astype(BF16)


def forward_body(part, r0, r1, r2, w_a, w_b, activated, slope, own, near, far):
    preact = part[...]
    for r in (r0, r1, r2):
        preact = preact + r[...].astype(F32)
    value, slope[...] = gelu_both(preact)
    hidden = value.astype(BF16)
    activated[...] = hidden
    outward(False, hidden, w_a, w_b, own, near, far)


def backward_body(part, r0, r1, r2, slope, w_a, w_b, grad_pre, own, near, far):
    grad = part[...]
    for r in (r0, r1, r2):
        grad = grad + r[...].astype(F32)
    hidden = (grad * slope[...]).astype(BF16)
    grad_pre[...] = hidden
    outward(True, hidden, w_a, w_b, own, near, far)


def call(body, values, outs, flops=0):
    vmem = pl.BlockSpec(memory_space=pltpu.VMEM)
    return pl.pallas_call(
        body,
        out_shape=[jax.ShapeDtypeStruct(shape, dtype) for shape, dtype in outs],
        in_specs=[vmem] * len(values),
        out_specs=[vmem] * len(outs),
        compiler_params=pltpu.CompilerParams(vmem_limit_bytes=32 * 2**20),
        cost_estimate=pl.CostEstimate(flops=flops, bytes_accessed=0, transcendentals=0),
    )(*values)


def on_device(tokens, cotangent, w_in, w_out):
    width, units = w_in.shape
    mine = jnp.stack([tokens, cotangent])
    block = jnp.concatenate([mine, send(mine, OTHER_CORE)], axis=1)
    slots = {i: send(block, Z_SLOTS[i]) for i in (3, 2, 1, 0)}
    slots = [slots[i] for i in range(4)]
    w_in_other = send(after(w_in, slots[1]), OTHER_CORE)
    w_out_other = send(after(w_out, slots[2]), OTHER_CORE)
    share = jnp.concatenate(slots, axis=1)
    across = send(share, OTHER_CORE)
    both = jnp.concatenate([share, across], axis=1)

    x_pieces = gather_x(share[0], both[0])
    rows, hidden_shape = 4 * share.shape[1], (4 * share.shape[1], 2 * units)
    outgoing = [((rows // 4, width), F32), ((rows // 2, width), BF16), ((rows // 4, width), BF16)]
    g_near = send(both[1], X_NEXT)
    hidden_out = [(hidden_shape, F32), (hidden_shape, BF16)]

    inner_part, rounded = call(
        functools.partial(inward, False), x_pieces + [w_in, w_in_other], hidden_out, FLOPS
    )
    inner_rest = exchange_rows(rounded)
    g_near = after(g_near, inner_part)
    g_pieces = [share[1], g_near, send(g_near[: share.shape[1]], X_NEXT)]
    back_part, rounded = call(
        functools.partial(inward, True), g_pieces + [w_out, w_out_other], hidden_out
    )
    back_rest = exchange_rows(rounded)

    inner_rest = [after(piece, back_part) for piece in inner_rest]
    activated, slope, forward, near, far = call(
        forward_body, [inner_part] + inner_rest + [w_out, w_out_other],
        [(hidden_shape, BF16), (hidden_shape, F32)] + outgoing,
    )
    forward_rest = send(near, inverse(X_NEXT)), send(far, inverse(X_FAR))
    grad_pre, backward, near, far = call(
        backward_body, [back_part] + back_rest + [slope, w_in, w_in_other],
        [(hidden_shape, BF16)] + outgoing,
    )
    backward_rest = send(near, inverse(X_NEXT)), send(far, inverse(X_FAR))
    forward = finish_x(forward, [after(piece, backward) for piece in forward_rest])

    x_rest, g_rest = (rows_of(pieces[1:]) for pieces in (x_pieces, g_pieces))
    rest = [
        rows_of([kept, columns_of(split_rows(hidden[:, units:], 8))])
        for kept, hidden in ((x_rest, grad_pre), (g_rest, activated))
    ]
    rest = send(jnp.stack(rest), OTHER_CORE)
    kept = x_rest.shape[0]

    def with_other(share, mine, across, hidden, other):
        hidden_other = rows_of([other[kept:, i * units : (i + 1) * units] for i in range(8)])
        return rows_of([share, mine, across, other[:kept]]), rows_of([hidden[:, :units], hidden_other])

    x_whole, pre_whole = with_other(share[0], x_rest, across[0], grad_pre, rest[0])
    g_whole, act_whole = with_other(share[1], g_rest, across[1], activated, rest[1])
    w_out_grad = t_dot(act_whole, g_whole).astype(BF16)
    w_in_grad = t_dot(x_whole, pre_whole).astype(BF16)

    backward_rest = [after(piece, w_in_grad, w_out_grad, forward) for piece in backward_rest]
    backward = finish_x(backward, backward_rest)
    result = jnp.stack([forward, backward])
    summed = jnp.zeros((2, 8, width), F32)
    for i in (1, 2, 0, 3):
        piece = send(result[:, 8 * i : 8 * i + 8], inverse(Z_SLOTS[i]))
        summed = summed + piece.astype(F32)
    summed = summed[:, :4] + send(summed[:, 4:].astype(BF16), OTHER_CORE).astype(F32)
    layer_output, input_grad = summed[0].astype(BF16), summed[1].astype(BF16)
    return (layer_output, input_grad, w_in_grad, w_out_grad)


def solution(mesh):
    in_specs = (
        P(PLANE, "row"),
        P(PLANE, "row"),
        P("row", PLANE),
        P(PLANE, "row"),
    )
    out_specs = (
        P(PLANE, "row"),
        P(PLANE, "row"),
        P("row", PLANE),
        P(PLANE, "row"),
    )
    return jax.shard_map(
        on_device, mesh=mesh, in_specs=in_specs, out_specs=out_specs, check_vma=False
    )
```

```python
import functools

import jax
import jax.numpy as jnp
from jax import lax
from jax.experimental import pallas as pl
from jax.experimental.pallas import tpu as pltpu
from jax.sharding import PartitionSpec as P

SQRT_TWO_PI = 0.7978845608028654
CUBIC = 0.044715
PLANE = ("dp", "col")
NX, NZ, NC = 4, 8, 2
BF16, F32 = jnp.bfloat16, jnp.float32
FLOPS = 4 * 10**9


def place(flat):
    dp, z_hi = divmod(flat, 4)
    return dp // 4, z_hi * 2 + (dp // 2) % 2, dp % 2


def index(x, z, core):
    x, z, core = x % NX, z % NZ, core % NC
    return ((x * 2 + z % 2) * 2 + core) * 4 + z // 2


def pairs(source_of):
    return [(index(*source_of(*place(f))), f) for f in range(NX * NZ * NC)]


def inverse(perm):
    return [(b, a) for a, b in perm]


OTHER_CORE = pairs(lambda x, z, c: (x, z, c + 1))
Z_SLOTS = [pairs(lambda x, z, c: (x, z + 4 * c, c))] + [
    pairs(lambda x, z, c, d=d: (x, z + (d if c == 0 else -d), c)) for d in (1, 2, 3)
]
X_NEXT = pairs(lambda x, z, c: (x + 1 - 2 * c, z, c))
X_FAR = pairs(lambda x, z, c: (x + 2, z, c))
ROW_SHIFTS = [[(i, (i + d) % 4) for i in range(4)] for d in (2, 3, 1)]


def send(value, perm):
    return lax.ppermute(value, PLANE, perm)


def gelu_both(preact):
    tangent = jnp.tanh(SQRT_TWO_PI * (preact + CUBIC * preact * preact * preact))
    value = 0.5 * preact * (1.0 + tangent)
    slope = 0.5 * (1.0 + tangent) + 0.5 * preact * (1.0 - tangent * tangent) * SQRT_TWO_PI * (
        1.0 + 3.0 * CUBIC * preact * preact
    )
    return value, slope


def after(value, *others):
    return lax.optimization_barrier((value,) + others)[0]


def exchange_rows(rounded):
    return [lax.ppermute(rounded, "row", shift) for shift in ROW_SHIFTS]


def total(part, received):
    for piece in received:
        part = part + piece.astype(F32)
    return part


def gather_x(share, both):
    return [share, send(both, X_NEXT), send(share, X_FAR)]


def finish_x(own, back):
    near, far = back
    rows = own.shape[0]
    across = send(near[rows:], OTHER_CORE)
    return total(own, [near[:rows], far, across]).astype(BF16)


def dot(a, b):
    return jnp.dot(a, b, preferred_element_type=F32)


def dot_t(a, b):
    return lax.dot_general(a, b, (((1,), (1,)), ((), ())), preferred_element_type=F32)


def t_dot(a, b):
    return lax.dot_general(a, b, (((0,), (0,)), ((), ())), preferred_element_type=F32)


def columns_of(pieces):
    return jnp.concatenate(pieces, axis=1)


def split_rows(value, count):
    rows = value.shape[0] // count
    return [value[i * rows : (i + 1) * rows] for i in range(count)]


def rows_of(pieces):
    return jnp.concatenate(pieces, axis=0)


CHUNK = 3072


def cuts(size):
    return [slice(k, k + CHUNK) for k in range(0, size, CHUNK)]


def inward(transposed, own, near, far, w_a, w_b, part, rounded):
    units = part.shape[1] // 2
    for i, w in enumerate((w_a, w_b)):
        total = 0.0
        for cut in cuts(own.shape[1]):
            rows = rows_of([own[:, cut], near[:, cut], far[:, cut]])
            total = total + (dot_t(rows, w[:, cut]) if transposed else dot(rows, w[cut, :]))
        columns = slice(i * units, (i + 1) * units)
        part[:, columns] = total
        rounded[:, columns] = total.astype(BF16)


def outward(transposed, hidden, w_a, w_b, own, near, far):
    units = hidden.shape[1] // 2
    a, b = hidden[:, :units], hidden[:, units:]
    n_own, n_near = own.shape[0], near.shape[0]
    for cut in cuts(own.shape[1]):
        if transposed:
            out = dot_t(a, w_a[cut, :]) + dot_t(b, w_b[cut, :])
        else:
            out = dot(a, w_a[:, cut]) + dot(b, w_b[:, cut])
        own[:, cut] = out[:n_own]
        near[:, cut] = out[n_own : n_own + n_near].astype(BF16)
        far[:, cut] = out[n_own + n_near :].astype(BF16)


def forward_body(part, r0, r1, r2, w_a, w_b, activated, slope, own, near, far):
    preact = part[...]
    for r in (r0, r1, r2):
        preact = preact + r[...].astype(F32)
    value, slope[...] = gelu_both(preact)
    hidden = value.astype(BF16)
    activated[...] = hidden
    outward(False, hidden, w_a, w_b, own, near, far)


def backward_body(part, r0, r1, r2, slope, w_a, w_b, grad_pre, own, near, far):
    grad = part[...]
    for r in (r0, r1, r2):
        grad = grad + r[...].astype(F32)
    hidden = (grad * slope[...]).astype(BF16)
    grad_pre[...] = hidden
    outward(True, hidden, w_a, w_b, own, near, far)


def call(body, values, outs, flops=0):
    vmem = pl.BlockSpec(memory_space=pltpu.VMEM)
    return pl.pallas_call(
        body,
        out_shape=[jax.ShapeDtypeStruct(shape, dtype) for shape, dtype in outs],
        in_specs=[vmem] * len(values),
        out_specs=[vmem] * len(outs),
        compiler_params=pltpu.CompilerParams(vmem_limit_bytes=32 * 2**20),
        cost_estimate=pl.CostEstimate(flops=flops, bytes_accessed=0, transcendentals=0),
    )(*values)


def on_device(tokens, cotangent, w_in, w_out):
    width, units = w_in.shape
    mine = jnp.stack([tokens, cotangent])
    block = jnp.concatenate([mine, send(mine, OTHER_CORE)], axis=1)
    slots = {i: send(block, Z_SLOTS[i]) for i in (3, 2, 1, 0)}
    slots = [slots[i] for i in range(4)]
    w_in_other = send(after(w_in, slots[1]), OTHER_CORE)
    w_out_other = send(after(w_out, slots[2]), OTHER_CORE)
    share = jnp.concatenate(slots, axis=1)
    across = send(share, OTHER_CORE)
    both = jnp.concatenate([share, across], axis=1)

    x_pieces = gather_x(share[0], both[0])
    rows, hidden_shape = 4 * share.shape[1], (4 * share.shape[1], 2 * units)
    outgoing = [((rows // 4, width), F32), ((rows // 2, width), BF16), ((rows // 4, width), BF16)]
    g_near = send(both[1], X_NEXT)
    hidden_out = [(hidden_shape, F32), (hidden_shape, BF16)]

    inner_part, rounded = call(
        functools.partial(inward, False), x_pieces + [w_in, w_in_other], hidden_out, FLOPS
    )
    inner_rest = exchange_rows(rounded)
    g_near = after(g_near, inner_part)
    g_pieces = [share[1], g_near, send(g_near[: share.shape[1]], X_NEXT)]
    back_part, rounded = call(
        functools.partial(inward, True), g_pieces + [w_out, w_out_other], hidden_out
    )
    back_rest = exchange_rows(rounded)

    inner_rest = [after(piece, back_part) for piece in inner_rest]
    activated, slope, forward, near, far = call(
        forward_body, [inner_part] + inner_rest + [w_out, w_out_other],
        [(hidden_shape, BF16), (hidden_shape, F32)] + outgoing,
    )
    forward_rest = send(near, inverse(X_NEXT)), send(far, inverse(X_FAR))
    grad_pre, backward, near, far = call(
        backward_body, [back_part] + back_rest + [slope, w_in, w_in_other],
        [(hidden_shape, BF16)] + outgoing,
    )
    backward_rest = send(near, inverse(X_NEXT)), send(far, inverse(X_FAR))
    forward = finish_x(forward, [after(piece, backward) for piece in forward_rest])

    x_rest, g_rest = (rows_of(pieces[1:]) for pieces in (x_pieces, g_pieces))
    rest = [
        rows_of([kept, columns_of(split_rows(hidden[:, units:], 8))])
        for kept, hidden in ((x_rest, grad_pre), (g_rest, activated))
    ]
    rest = send(jnp.stack(rest), OTHER_CORE)
    kept = x_rest.shape[0]

    def with_other(share, mine, across, hidden, other):
        hidden_other = rows_of([other[kept:, i * units : (i + 1) * units] for i in range(8)])
        return rows_of([share, mine, across, other[:kept]]), rows_of([hidden[:, :units], hidden_other])

    x_whole, pre_whole = with_other(share[0], x_rest, across[0], grad_pre, rest[0])
    g_whole, act_whole = with_other(share[1], g_rest, across[1], activated, rest[1])
    w_out_grad = t_dot(act_whole, g_whole).astype(BF16)
    w_in_grad = t_dot(x_whole, pre_whole).astype(BF16)

    backward_rest = [after(piece, w_in_grad, w_out_grad, forward) for piece in backward_rest]
    backward = finish_x(backward, backward_rest)
    result = jnp.stack([forward, backward])
    summed = jnp.zeros((2, 8, width), F32)
    for i in (1, 2, 0, 3):
        piece = send(result[:, 8 * i : 8 * i + 8], inverse(Z_SLOTS[i]))
        summed = summed + piece.astype(F32)
    summed = summed[:, :4] + send(summed[:, 4:].astype(BF16), OTHER_CORE).astype(F32)
    layer_output, input_grad = summed[0].astype(BF16), summed[1].astype(BF16)
    return (layer_output, input_grad, w_in_grad, w_out_grad)


def solution(mesh):
    in_specs = (
        P(PLANE, "row"),
        P(PLANE, "row"),
        P("row", PLANE),
        P(PLANE, "row"),
    )
    out_specs = (
        P(PLANE, "row"),
        P(PLANE, "row"),
        P("row", PLANE),
        P(PLANE, "row"),
    )
    return jax.shard_map(
        on_device, mesh=mesh, in_specs=in_specs, out_specs=out_specs, check_vma=False
    )
```
